32 devices in a mesh: space: 8 (over y, x, core), date: 4 (over z).
Axes of the slice: x: 2, y: 2, z: 4, core: 2. Of those that a mesh axis runs over, the one named last changes fastest.
Arguments:
- scene_panels: float32 [4, 64, 48, 384], P('date', 'space'), may hold values from -25 to 25
- panel_owner: int32 [4, 64], P('date'), may hold values from 0 to 7, as said below
- panel_offset: int32 [4, 64], P('date'), may hold values from 0 to 7, as said below
- panel_rows: int32 [4, 64], P('date'), may hold values from 24 to 48
- pair_used: int32 [4, 2], P('date'), may hold values 0 or 1
Outputs:
- correlation: float32 [4, 8, 2, 17, 17, 144], P('date', 'space')
The draws below stay inside these ranges and needn't reach their ends.
Inputs may be any that keep to these rules, and one draw needn't show every extreme that they name: `panel_owner`: for each date, the 8 panels held by one index of space name each tile once. `panel_offset`: for each date and tile, the panels that name the tile carry each slot 0 to 7 once.
All inputs are finite; a program needn't handle non-finite values. No bound on the sum of `pair_used` on one device may be relied on, other than what follows from the above.
Results may differ from the reference program's by a relative error of at most 0.0028.
Values may be sent and summed in bfloat16 or wider, within the bound.
A program may use at most 64 MiB of HBM per device.

```python
import jax
import jax.numpy as jnp
from jax import lax

TILE = 384
CHIP = 32
SEARCH = 8
WALLIS = 10
NTILES = 8
NDATES = 4
SHIFTS = 2
PANEL_ROWS = 48
PANELS = 64
FRAME = 48
LAGS = 17
CHIPS = 144


def footprints(key):
    key = jax.random.fold_in(key, 101)
    first, second = jax.random.split(key)
    owner_keys = jax.random.split(first, NDATES * NTILES)
    owner = jax.vmap(lambda single: jax.random.permutation(single, NTILES))(owner_keys)
    owner = owner.reshape(NDATES, PANELS).astype(jnp.int32)
    slot_keys = jax.random.split(second, NDATES * NTILES)
    slots = jax.vmap(lambda single: jax.random.permutation(single, NTILES))(slot_keys)
    slots = slots.reshape(NDATES, NTILES, NTILES).astype(jnp.int32)
    source = (jnp.arange(PANELS) // NTILES).astype(jnp.int32)
    dates = jnp.arange(NDATES).astype(jnp.int32)[:, None]
    offset = slots[dates, owner, source[None, :]]
    return (owner, offset.astype(jnp.int32))


def draw_panel_owner(key, part):
    shared = footprints(key)
    return shared[0]


def draw_panel_offset(key, part):
    shared = footprints(key)
    return shared[1]


def moved(texture, row_index, col_index):
    return texture[row_index][:, col_index]


def draw_scene_panels(key, part):
    owner, offset = footprints(key)
    key = jax.random.fold_in(key, 7)
    key_texture, key_noise, key_speed = jax.random.split(key, 3)
    texture = jnp.clip(jax.random.normal(key_texture, (NTILES, TILE, TILE), jnp.float32), -5.0, 5.0)
    speed = jax.random.randint(key_speed, (NTILES, 2), -2, 3).astype(jnp.int32)
    pixels = jnp.arange(TILE).astype(jnp.int32)
    dates = jnp.arange(NDATES).astype(jnp.int32)
    shift_rows = (pixels[None, None, :] + dates[:, None, None] * speed[None, :, 0:1]) % TILE
    shift_cols = (pixels[None, None, :] + dates[:, None, None] * speed[None, :, 1:2]) % TILE
    images = jax.vmap(jax.vmap(moved, in_axes=(0, 0, 0)), in_axes=(None, 0, 0))(texture, shift_rows, shift_cols)
    noise = 0.5 * jnp.clip(jax.random.normal(key_noise, (NDATES, NTILES, TILE, TILE), jnp.float32), -5.0, 5.0)
    scene = 0.8 * images + noise
    scene = scene.reshape(NDATES, NTILES, NTILES, PANEL_ROWS, TILE)
    date_index = jnp.arange(NDATES).astype(jnp.int32)[:, None]
    return scene[date_index, owner, offset]


def with_ends(entries, stream_key, smallest, high):
    longest = entries.shape.index(max(entries.shape))
    spots = []
    for shift in (0, 1):
        where = [jax.random.randint(jax.random.fold_in(stream_key, axis), (), 0, length) for axis, length in enumerate(entries.shape)]
        where[longest] = (where[longest] + shift) % entries.shape[longest]
        spots.append(tuple(where))
    return entries.at[spots[0]].set(smallest).at[spots[1]].set(high)


def setup_inputs(seed: int = 0) -> dict:
    seeds = jax.random.split(jax.random.key(seed), 6)
    return {
        "scene_panels": draw_scene_panels(jax.random.fold_in(seeds[5], 71), 0),
        "panel_owner": draw_panel_owner(jax.random.fold_in(seeds[5], 71), 0),
        "panel_offset": draw_panel_offset(jax.random.fold_in(seeds[5], 71), 0),
        "panel_rows": with_ends(jax.random.randint(seeds[3], (NDATES, PANELS), PANEL_ROWS // 2, PANEL_ROWS + 1), jax.random.fold_in(seeds[3], 1), PANEL_ROWS // 2, PANEL_ROWS).astype(jnp.int32),
        "pair_used": with_ends((jax.random.randint(seeds[4], (NDATES, SHIFTS), 0, 4) < 3).astype(jnp.int32), jax.random.fold_in(seeds[4], 1), 0, 1),
    }


WALLIS_FLOOR = 0.25
MATCH_FLOOR = 0.1

def banded(size, radius):
    index = jnp.arange(size)
    return (jnp.abs(index[:, None] - index[None, :]) <= radius).astype(jnp.float32)

def wallis(image):
    exact = lax.Precision.HIGHEST
    box = banded(image.shape[0], WALLIS)
    counts = lax.optimization_barrier(jnp.sum(box, axis=1))
    area = counts[:, None] * counts[None, :]
    total = jnp.dot(jnp.dot(box, image, precision=exact), box, precision=exact)
    squares = jnp.dot(jnp.dot(box, image * image, precision=exact), box, precision=exact)
    center = total / area
    spread = squares / area - center * center
    return ((image - center) / jnp.sqrt(spread + WALLIS_FLOOR)).astype(jnp.bfloat16)

def assemble(panels, owner, offset, rows):
    live = (jnp.arange(PANEL_ROWS)[None, :] < rows[:, None]).astype(jnp.float32)
    masked = panels * live[:, :, None]
    slot_ids = owner * NTILES + offset
    placed = jnp.zeros_like(masked).at[slot_ids].set(masked)
    return placed.reshape(NTILES, TILE, TILE)

def frames_of(image):
    count = TILE // CHIP
    padded = jnp.pad(image, SEARCH)
    starts = CHIP * jnp.arange(count)[:, None] + jnp.arange(FRAME)[None, :]
    windows = padded[starts[:, None, :, None], starts[None, :, None, :]]
    return windows.reshape(count * count, FRAME, FRAME)

def chips_of(image):
    count = TILE // CHIP
    blocks = image.reshape(count, CHIP, count, CHIP).transpose(0, 2, 1, 3).reshape(count * count, CHIP, CHIP)
    return jnp.pad(blocks, ((0, 0), (0, FRAME - CHIP), (0, FRAME - CHIP)))

def correlate(own, other, used):
    refs = chips_of(own)
    frames = frames_of(other)
    spectrum = jnp.conj(jnp.fft.rfft2(refs)) * jnp.fft.rfft2(frames)
    raw = jnp.fft.irfft2(spectrum, s=(FRAME, FRAME))[:, :LAGS, :LAGS]
    lag_index = jnp.arange(LAGS)[:, None]
    pixel_index = jnp.arange(FRAME)[None, :]
    band = ((pixel_index >= lag_index) & (pixel_index < lag_index + CHIP)).astype(jnp.float32)
    energy = jnp.einsum('ua,cab,vb->cuv', band, frames * frames, band, precision=lax.Precision.HIGHEST)
    area = float(CHIP * CHIP)
    ref_power = lax.optimization_barrier(jnp.sum(refs * refs, axis=(1, 2))) / area
    match = raw / area / jnp.sqrt((ref_power[:, None, None] + MATCH_FLOOR) * (energy / area + MATCH_FLOOR))
    return (match * used).transpose(1, 2, 0)

def reference(scene_panels, panel_owner, panel_offset, panel_rows, pair_used):

    def per_date(date):
        tiles = assemble(scene_panels[date], panel_owner[date], panel_offset[date], panel_rows[date])
        return lax.map(wallis, tiles)
    filtered = lax.map(per_date, jnp.arange(NDATES))

    def per_pair(index):
        date = index // NTILES
        tile = index % NTILES
        own = filtered[date, tile].astype(jnp.float32)
        surfaces = []
        for shift in range(1, SHIFTS + 1):
            other = filtered[(date - shift) % NDATES, tile].astype(jnp.float32)
            surfaces.append(correlate(own, other, pair_used[date, shift - 1].astype(jnp.float32)))
        return jnp.stack(surfaces)
    result = lax.map(per_pair, jnp.arange(NDATES * NTILES))
    return result.reshape(NDATES, NTILES, SHIFTS, LAGS, LAGS, CHIPS)
```

```python
import functools
import math

import jax
import jax.numpy as jnp
import ml_dtypes
import numpy as np
from jax import lax
from jax.experimental import pallas as pl
from jax.experimental.pallas import tpu as pltpu
from jax.sharding import PartitionSpec as P

CHIP = 32
SEARCH = 8
WALLIS = 10
FRAME = CHIP + 2 * SEARCH
LAGS = 2 * SEARCH + 1
HALF = FRAME // 2
WALLIS_FLOOR = 0.25
MATCH_FLOOR = 0.1
TILE = 384
COUNT = TILE // CHIP
CHIPS = COUNT * COUNT
GROUPS = 3
PER = COUNT // GROUPS
UPAD = 24
FIRST = 128 // COUNT
F32 = jnp.float32
BF16 = jnp.bfloat16

ROW_START = (0, 112, 224)
ROW_LEN = 160
COL_START = (0, 0, 128)
COL_LEN = (256, 384, 256)


def lane_of(v, cj):
    return v * COUNT + cj if v < FIRST else 128 + (v - FIRST) * COUNT + cj


def split_host(x):
    hi = x.astype(ml_dtypes.bfloat16)
    lo = (x - hi.astype(np.float64)).astype(ml_dtypes.bfloat16)
    return np.stack([hi, lo])


@functools.lru_cache(None)
def tables():
    j = np.arange(HALF)
    omega = 2.0 * math.pi * (j + 0.5) / FRAME

    def columns(lo, hi):
        out = np.zeros((TILE, GROUPS * 256))
        for cj in range(COUNT):
            g, q = divmod(cj, PER)
            for b in range(lo, hi):
                x = CHIP * cj + b - SEARCH
                if 0 <= x < TILE:
                    base = g * 256 + q * HALF
                    out[x, base : base + HALF] = np.cos(omega * (b - lo if lo else b))
                    out[x, base + 128 : base + 128 + HALF] = np.sin(omega * (b - lo if lo else b))
        return out

    def rows(lo, hi):
        out = np.zeros((GROUPS, 2 * PER * HALF, ROW_LEN))
        for ci in range(COUNT):
            h, q = divmod(ci, PER)
            for a in range(lo, hi):
                y = CHIP * ci + a - SEARCH
                if 0 <= y < TILE:
                    out[h, q * HALF : (q + 1) * HALF, y - ROW_START[h]] = np.cos(omega * (a - lo if lo else a))
                    base = PER * HALF + q * HALF
                    out[h, base : base + HALF, y - ROW_START[h]] = np.sin(omega * (a - lo if lo else a))
        return out

    back_rows = np.zeros((PER * UPAD, 2 * PER * HALF))
    for q in range(PER):
        for u in range(LAGS):
            back_rows[q * UPAD + u, q * HALF : (q + 1) * HALF] = np.cos(omega * u)
            base = PER * HALF + q * HALF
            back_rows[q * UPAD + u, base : base + HALF] = np.sin(omega * u)
    back_cols = np.zeros((GROUPS, 256, 256))
    for cj in range(COUNT):
        g, q = divmod(cj, PER)
        for v in range(LAGS):
            back_cols[g, q * HALF : (q + 1) * HALF, lane_of(v, cj)] = np.cos(omega * v)
            base = 128 + q * HALF
            back_cols[g, base : base + HALF, lane_of(v, cj)] = np.sin(omega * v)

    wide = np.zeros((2, TILE, 256))
    tall = np.zeros((2, COUNT * UPAD, TILE))
    for c in range(COUNT):
        for v in range(LAGS):
            start = CHIP * c + v - SEARCH
            wide[0, max(start, 0) : max(start + CHIP, 0), lane_of(v, c)] = 1
            tall[0, c * UPAD + v, max(start, 0) : max(start + CHIP, 0)] = 1
            wide[1, CHIP * c : CHIP * c + CHIP, lane_of(v, c)] = 1
            tall[1, c * UPAD + v, CHIP * c : CHIP * c + CHIP] = 1
    return (
        split_host(columns(SEARCH, SEARCH + CHIP)),
        split_host(columns(0, FRAME)),
        split_host(rows(SEARCH, SEARCH + CHIP)),
        split_host(rows(0, FRAME)),
        split_host(back_rows),
        split_host(back_cols),
        wide.astype(ml_dtypes.bfloat16),
        tall.astype(ml_dtypes.bfloat16),
    )


def dot(a, b):
    return jnp.dot(a, b, preferred_element_type=F32)


def split(x):
    hi = x.astype(BF16)
    return hi, (x - hi.astype(F32)).astype(BF16)


def split3(x):
    hi = x.astype(BF16)
    rest = x - hi.astype(F32)
    mid = rest.astype(BF16)
    return hi, mid, (rest - mid.astype(F32)).astype(BF16)


def boxed(x, box):
    a, b, c = split3(x)
    first = dot(box, a) + dot(box, b) + dot(box, c)
    a, b, c = split3(first)
    return dot(a, box) + dot(b, box) + dot(c, box)


def wallis(image):
    size = image.shape[0]
    i = lax.broadcasted_iota(jnp.int32, (size, size), 0)
    j = lax.broadcasted_iota(jnp.int32, (size, size), 1)
    box = jnp.where(jnp.abs(i - j) <= WALLIS, 1.0, 0.0).astype(BF16)

    def counts(k):
        return (jnp.minimum(k, WALLIS) + jnp.minimum(size - 1 - k, WALLIS) + 1).astype(F32)

    rows = counts(lax.broadcasted_iota(jnp.int32, (size, 1), 0))
    cols = counts(lax.broadcasted_iota(jnp.int32, (1, size), 1))
    inverse = (1.0 / rows) * (1.0 / cols)
    center = boxed(image, box) * inverse
    spread = boxed(image * image, box) * inverse - center * center
    return ((image - center) * lax.rsqrt(spread + WALLIS_FLOOR)).astype(BF16)


def wallis_kernel(image_ref, out_ref):
    out_ref[...] = wallis(image_ref[...])


def spectrum(x, cols_ref, rows_ref, store):
    parts = []
    for g in range(GROUPS):
        at = pl.ds(COL_START[g], COL_LEN[g])
        piece = x[:, COL_START[g] : COL_START[g] + COL_LEN[g]]
        lanes = pl.ds(g * 256, 256)
        z = dot(piece, cols_ref[0, at, lanes]) + dot(piece, cols_ref[1, at, lanes])
        hi, lo = split(z)
        for h in range(GROUPS):
            s = ROW_START[h]
            zh, zl = hi[s : s + ROW_LEN], lo[s : s + ROW_LEN]
            store[h, :, lanes] = dot(rows_ref[0, h], zh) + dot(rows_ref[0, h], zl) + dot(rows_ref[1, h], zh)


def powers(x, wide, tall):
    wide_f = x.astype(F32)
    hi, lo = split(wide_f * wide_f)
    hi, lo = split(dot(hi, wide) + dot(lo, wide))
    return dot(tall, hi) + dot(tall, lo)


def surfaces(ref_spec, frame_spec, ref_power, frame_power, used, back_rows, back_cols, match_ref):
    mid = PER * HALF
    area = float(CHIP * CHIP)
    for h in range(GROUPS):
        total = None
        for g in range(GROUPS):
            even, odd = pl.ds(g * 256, 128), pl.ds(g * 256 + 128, 128)
            top, low = pl.ds(0, mid), pl.ds(mid, mid)
            rcc, rcs = ref_spec[h, top, even], ref_spec[h, top, odd]
            rsc, rss = ref_spec[h, low, even], ref_spec[h, low, odd]
            wcc, wcs = frame_spec[h, top, even], frame_spec[h, top, odd]
            wsc, wss = frame_spec[h, low, even], frame_spec[h, low, odd]
            ap, bp, am, bm = rcc - rss, rsc + rcs, rcc + rss, rsc - rcs
            cp, dp, cm, dm = wcc - wss, wsc + wcs, wcc + wss, wsc - wcs
            pr, pi = ap * cp + bp * dp, bp * cp - ap * dp
            mr, mi = am * cm + bm * dm, bm * cm - am * dm
            upper = jnp.concatenate([pr + mr, mi - pi], axis=1)
            lower = jnp.concatenate([-(pi + mi), mr - pr], axis=1)
            hi, lo = split(jnp.concatenate([upper, lower], axis=0))
            y = dot(back_rows[0], hi) + dot(back_rows[0], lo) + dot(back_rows[1], hi)
            hi, lo = split(y)
            term = dot(hi, back_cols[0, g]) + dot(lo, back_cols[0, g]) + dot(hi, back_cols[1, g])
            total = term if total is None else total + term
        at = pl.ds(h * PER * UPAD, PER * UPAD)
        scale = 2.0 / (FRAME * FRAME) / area
        power = (ref_power[at, :] * (1.0 / area) + MATCH_FLOOR) * (frame_power[at, :] * (1.0 / area) + MATCH_FLOOR)
        match_ref[at, :] = total * (scale * used) * lax.rsqrt(power)


def arrange(match_ref, out_ref, k):
    lane = lax.broadcasted_iota(jnp.int32, (UPAD, 128), 1)
    for v in range(LAGS):
        start = lane_of(v, 0)
        tile, off = divmod(start, 128)
        first = jnp.zeros((UPAD, 128), F32)
        second = jnp.zeros((UPAD, 128), F32)
        for ci in range(COUNT):
            piece = match_ref[pl.ds(ci * UPAD, UPAD), pl.ds(tile * 128, 128)]
            turn = (COUNT * ci - off) % 128
            if turn:
                piece = pltpu.roll(piece, turn, 1)
            begin, end = COUNT * ci, COUNT * ci + COUNT
            if begin < 128:
                first = jnp.where((lane >= begin) & (lane < end), piece, first)
            if end > 128:
                second = jnp.where((lane >= begin - 128) & (lane < end - 128), piece, second)
        out_ref[k, :, v, pl.ds(0, 128)] = first[:LAGS]
        out_ref[k, :, v, pl.ds(128, CHIPS - 128)] = second[:LAGS, : CHIPS - 128]


def correlate_kernel(
    used_ref, own_ref, one_ref, two_ref,
    ref_cols, frame_cols, ref_rows, frame_rows, back_rows, back_cols, wide, tall,
    out_ref, ref_spec, frame_spec, ref_power, frame_power, match_ref,
):
    own = own_ref[...]
    spectrum(own, ref_cols, ref_rows, ref_spec)
    ref_power[...] = powers(own, wide[1], tall[1])
    for k, held in enumerate((one_ref, two_ref)):
        x = held[...]
        spectrum(x, frame_cols, frame_rows, frame_spec)
        frame_power[...] = powers(x, wide[0], tall[0])
        used = used_ref[k].astype(F32)
        surfaces(ref_spec, frame_spec, ref_power, frame_power, used, back_rows, back_cols, match_ref)
        arrange(match_ref, out_ref, k)


def shifted(x, axis, by):
    devices = lax.axis_size(axis)
    return lax.ppermute(x, axis, [(i, (i + by) % devices) for i in range(devices)])


def local(scene_panels, panel_owner, panel_offset, panel_rows, pair_used):
    tiles = lax.axis_size("space")
    here = lax.axis_index("space")
    panels = scene_panels[0]
    rows_each = panels.shape[1]
    width = panels.shape[2]
    owner = panel_owner[0].reshape(tiles, tiles)
    offset = panel_offset[0].reshape(tiles, tiles)
    valid = panel_rows[0].reshape(tiles, tiles)
    mine = owner[here]
    live = (jnp.arange(rows_each)[None, :] < valid[here][:, None]).astype(jnp.float32)
    masked = panels * live[:, :, None]
    targets = jnp.arange(tiles, dtype=jnp.int32)
    picks = jnp.sum(jnp.where(mine[None, :] == targets[:, None], targets[None, :], 0), axis=1)
    outgoing = masked[picks]
    incoming = lax.all_to_all(outgoing, "space", split_axis=0, concat_axis=0, tiled=True)
    slot_of = jnp.sum(jnp.where(owner == here, offset, 0), axis=1)
    order = jnp.sum(jnp.where(slot_of[None, :] == targets[:, None], targets[None, :], 0), axis=1)
    image = incoming[order].reshape(width, width)
    vmem = pl.BlockSpec(memory_space=pltpu.VMEM)
    filtered = pl.pallas_call(
        wallis_kernel,
        out_shape=jax.ShapeDtypeStruct((width, width), BF16),
        in_specs=[vmem],
        out_specs=vmem,
        compiler_params=pltpu.CompilerParams(vmem_limit_bytes=40 * 2**20),
    )(image)
    one = shifted(filtered, "date", 1)
    two = shifted(filtered, "date", 2)
    consts = [jnp.asarray(t) for t in tables()]
    shifts = pair_used.shape[1]
    out = pl.pallas_call(
        correlate_kernel,
        out_shape=jax.ShapeDtypeStruct((shifts, LAGS, LAGS, CHIPS), F32),
        in_specs=[pl.BlockSpec(memory_space=pltpu.SMEM)] + [vmem] * (3 + len(consts)),
        out_specs=vmem,
        scratch_shapes=[
            pltpu.VMEM((GROUPS, 2 * PER * HALF, GROUPS * 256), F32),
            pltpu.VMEM((GROUPS, 2 * PER * HALF, GROUPS * 256), F32),
            pltpu.VMEM((COUNT * UPAD, 256), F32),
            pltpu.VMEM((COUNT * UPAD, 256), F32),
            pltpu.VMEM((COUNT * UPAD, 256), F32),
        ],
        compiler_params=pltpu.CompilerParams(vmem_limit_bytes=40 * 2**20),
    )(pair_used[0], filtered, one, two, *consts)
    return out[None, None]


def solution(mesh):
    placed = (
        P("date", "space", None, None),
        P("date", None),
        P("date", None),
        P("date", None),
        P("date", None),
    )
    return jax.shard_map(
        local,
        mesh=mesh,
        in_specs=placed,
        out_specs=P("date", "space", None, None, None, None),
        check_vma=False,
    )
```

```python
import functools
import math

import jax
import jax.numpy as jnp
import ml_dtypes
import numpy as np
from jax import lax
from jax.experimental import pallas as pl
from jax.experimental.pallas import tpu as pltpu
from jax.sharding import PartitionSpec as P

CHIP = 32
SEARCH = 8
WALLIS = 10
FRAME = CHIP + 2 * SEARCH
LAGS = 2 * SEARCH + 1
HALF = FRAME // 2
WALLIS_FLOOR = 0.25
MATCH_FLOOR = 0.1
TILE = 384
COUNT = TILE // CHIP
CHIPS = COUNT * COUNT
GROUPS = 3
PER = COUNT // GROUPS
UPAD = 24
FIRST = 128 // COUNT
F32 = jnp.float32
BF16 = jnp.bfloat16
MESH = pl.DeviceIdType.MESH
TABLES = 8
CHUNKS = 3

ROW_START = (0, 112, 224)
ROW_LEN = 160
COL_START = (0, 0, 128)
COL_LEN = (256, 384, 256)


def lane_of(v, cj):
    return v * COUNT + cj if v < FIRST else 128 + (v - FIRST) * COUNT + cj


def split_host(x):
    hi = x.astype(ml_dtypes.bfloat16)
    lo = (x - hi.astype(np.float64)).astype(ml_dtypes.bfloat16)
    return np.stack([hi, lo])


@functools.lru_cache(None)
def tables():
    j = np.arange(HALF)
    omega = 2.0 * math.pi * (j + 0.5) / FRAME

    def columns(lo, hi):
        out = np.zeros((TILE, GROUPS * 256))
        for cj in range(COUNT):
            g, q = divmod(cj, PER)
            for b in range(lo, hi):
                x = CHIP * cj + b - SEARCH
                if 0 <= x < TILE:
                    base = g * 256 + q * HALF
                    out[x, base : base + HALF] = np.cos(omega * (b - lo if lo else b))
                    out[x, base + 128 : base + 128 + HALF] = np.sin(omega * (b - lo if lo else b))
        return out

    def rows(lo, hi):
        out = np.zeros((GROUPS, 2 * PER * HALF, ROW_LEN))
        for ci in range(COUNT):
            h, q = divmod(ci, PER)
            for a in range(lo, hi):
                y = CHIP * ci + a - SEARCH
                if 0 <= y < TILE:
                    out[h, q * HALF : (q + 1) * HALF, y - ROW_START[h]] = np.cos(omega * (a - lo if lo else a))
                    base = PER * HALF + q * HALF
                    out[h, base : base + HALF, y - ROW_START[h]] = np.sin(omega * (a - lo if lo else a))
        return out

    back_rows = np.zeros((PER * UPAD, 2 * PER * HALF))
    for q in range(PER):
        for u in range(LAGS):
            back_rows[q * UPAD + u, q * HALF : (q + 1) * HALF] = np.cos(omega * u)
            base = PER * HALF + q * HALF
            back_rows[q * UPAD + u, base : base + HALF] = np.sin(omega * u)
    back_cols = np.zeros((GROUPS, 256, 256))
    for cj in range(COUNT):
        g, q = divmod(cj, PER)
        for v in range(LAGS):
            back_cols[g, q * HALF : (q + 1) * HALF, lane_of(v, cj)] = np.cos(omega * v)
            base = 128 + q * HALF
            back_cols[g, base : base + HALF, lane_of(v, cj)] = np.sin(omega * v)

    wide = np.zeros((2, TILE, 256))
    tall = np.zeros((2, COUNT * UPAD, TILE))
    for c in range(COUNT):
        for v in range(LAGS):
            start = CHIP * c + v - SEARCH
            wide[0, max(start, 0) : max(start + CHIP, 0), lane_of(v, c)] = 1
            tall[0, c * UPAD + v, max(start, 0) : max(start + CHIP, 0)] = 1
            wide[1, CHIP * c : CHIP * c + CHIP, lane_of(v, c)] = 1
            tall[1, c * UPAD + v, CHIP * c : CHIP * c + CHIP] = 1
    return (
        split_host(columns(SEARCH, SEARCH + CHIP)),
        split_host(columns(0, FRAME)),
        split_host(rows(SEARCH, SEARCH + CHIP)),
        split_host(rows(0, FRAME)),
        split_host(back_rows),
        split_host(back_cols),
        wide.astype(ml_dtypes.bfloat16),
        tall.astype(ml_dtypes.bfloat16),
    )


def dot(a, b):
    return jnp.dot(a, b, preferred_element_type=F32)


def split(x):
    hi = x.astype(BF16)
    return hi, (x - hi.astype(F32)).astype(BF16)


def split3(x):
    hi = x.astype(BF16)
    rest = x - hi.astype(F32)
    mid = rest.astype(BF16)
    return hi, mid, (rest - mid.astype(F32)).astype(BF16)


def boxed(x, box):
    a, b, c = split3(x)
    return dot(a, box) + dot(b, box) + dot(c, box)


def banded(rows, first, size):
    i = lax.broadcasted_iota(jnp.int32, (rows, size), 0) + first
    j = lax.broadcasted_iota(jnp.int32, (rows, size), 1)
    return jnp.where(jnp.abs(i - j) <= WALLIS, 1.0, 0.0).astype(BF16)


def counts(k, size):
    return (jnp.minimum(k, WALLIS) + jnp.minimum(size - 1 - k, WALLIS) + 1).astype(F32)


def wallis(image_ref, filtered_ref, chunk, ready):
    size = image_ref.shape[0]
    image = image_ref[...]
    box = banded(size, 0, size)
    totals = split3(boxed(image, box))
    squares = split3(boxed(image * image, box))
    cols = 1.0 / counts(lax.broadcasted_iota(jnp.int32, (1, size), 1), size)
    for c in range(size // chunk):
        first = c * chunk
        part = banded(chunk, first, size)
        rows = 1.0 / counts(lax.broadcasted_iota(jnp.int32, (chunk, 1), 0) + first, size)
        inverse = rows * cols
        center = sum(dot(part, t) for t in totals) * inverse
        spread = sum(dot(part, t) for t in squares) * inverse - center * center
        at = pl.ds(first, chunk)
        filtered_ref[c] = ((image_ref[at, :] - center) * lax.rsqrt(spread + WALLIS_FLOOR)).astype(BF16)
        ready(c)


def spectrum(x, cols_ref, rows_ref, store):
    parts = []
    for g in range(GROUPS):
        at = pl.ds(COL_START[g], COL_LEN[g])
        piece = x[:, COL_START[g] : COL_START[g] + COL_LEN[g]]
        lanes = pl.ds(g * 256, 256)
        z = dot(piece, cols_ref[0, at, lanes]) + dot(piece, cols_ref[1, at, lanes])
        hi, lo = split(z)
        for h in range(GROUPS):
            s = ROW_START[h]
            zh, zl = hi[s : s + ROW_LEN], lo[s : s + ROW_LEN]
            store[h, :, lanes] = dot(rows_ref[0, h], zh) + dot(rows_ref[0, h], zl) + dot(rows_ref[1, h], zh)


def powers(x, wide, tall):
    wide_f = x.astype(F32)
    hi, lo = split(wide_f * wide_f)
    hi, lo = split(dot(hi, wide) + dot(lo, wide))
    return dot(tall, hi) + dot(tall, lo)


def surfaces(ref_spec, frame_spec, ref_power, frame_power, used, back_rows, back_cols, match_ref):
    mid = PER * HALF
    area = float(CHIP * CHIP)
    for h in range(GROUPS):
        total = None
        for g in range(GROUPS):
            even, odd = pl.ds(g * 256, 128), pl.ds(g * 256 + 128, 128)
            top, low = pl.ds(0, mid), pl.ds(mid, mid)
            rcc, rcs = ref_spec[h, top, even], ref_spec[h, top, odd]
            rsc, rss = ref_spec[h, low, even], ref_spec[h, low, odd]
            wcc, wcs = frame_spec[h, top, even], frame_spec[h, top, odd]
            wsc, wss = frame_spec[h, low, even], frame_spec[h, low, odd]
            ap, bp, am, bm = rcc - rss, rsc + rcs, rcc + rss, rsc - rcs
            cp, dp, cm, dm = wcc - wss, wsc + wcs, wcc + wss, wsc - wcs
            pr, pi = ap * cp + bp * dp, bp * cp - ap * dp
            mr, mi = am * cm + bm * dm, bm * cm - am * dm
            upper = jnp.concatenate([pr + mr, mi - pi], axis=1)
            lower = jnp.concatenate([-(pi + mi), mr - pr], axis=1)
            hi, lo = split(jnp.concatenate([upper, lower], axis=0))
            y = dot(back_rows[0], hi) + dot(back_rows[0], lo) + dot(back_rows[1], hi)
            hi, lo = split(y)
            term = dot(hi, back_cols[0, g]) + dot(lo, back_cols[0, g]) + dot(hi, back_cols[1, g])
            total = term if total is None else total + term
        at = pl.ds(h * PER * UPAD, PER * UPAD)
        scale = 2.0 / (FRAME * FRAME) / area
        power = (ref_power[at, :] * (1.0 / area) + MATCH_FLOOR) * (frame_power[at, :] * (1.0 / area) + MATCH_FLOOR)
        match_ref[at, :] = total * (scale * used) * lax.rsqrt(power)


def arrange(match_ref, out_ref, k):
    lane = lax.broadcasted_iota(jnp.int32, (UPAD, 128), 1)
    for v in range(LAGS):
        start = lane_of(v, 0)
        tile, off = divmod(start, 128)
        first = jnp.zeros((UPAD, 128), F32)
        second = jnp.zeros((UPAD, 128), F32)
        for ci in range(COUNT):
            piece = match_ref[pl.ds(ci * UPAD, UPAD), pl.ds(tile * 128, 128)]
            turn = (COUNT * ci - off) % 128
            if turn:
                piece = pltpu.roll(piece, turn, 1)
            begin, end = COUNT * ci, COUNT * ci + COUNT
            if begin < 128:
                first = jnp.where((lane >= begin) & (lane < end), piece, first)
            if end > 128:
                second = jnp.where((lane >= begin - 128) & (lane < end - 128), piece, second)
        out_ref[k, :, v, pl.ds(0, 128)] = first[:LAGS]
        out_ref[k, :, v, pl.ds(128, CHIPS - 128)] = second[:LAGS, : CHIPS - 128]


def whole_of(ref):
    return jnp.concatenate([ref[c] for c in range(ref.shape[0])], axis=0)


def kernel(
    tiles, dates,
    owner_ref, offset_ref, valid_ref, used_ref, panels_ref, *refs,
):
    hbm = refs[:TABLES]
    out_ref = refs[TABLES]
    held = refs[TABLES + 1 : 2 * TABLES + 1]
    (
        stage, recv, image_ref, own_ref, one_ref, two_ref,
        ref_spec, frame_spec, ref_power, frame_power, match_ref,
        table_sem, panel_send, panel_recv, one_send, one_recv, two_send, two_recv,
    ) = refs[2 * TABLES + 1 :]
    here = lax.axis_index("space")
    date = lax.axis_index("date")
    right, left = lax.rem(date + 1, dates), lax.rem(date + dates - 1, dates)
    loads = [pltpu.make_async_copy(hbm[i], held[i], table_sem.at[i]) for i in range(TABLES)]
    for load in loads:
        load.start()

    barrier = pltpu.get_barrier_semaphore()
    for step in range(1, tiles):
        pl.semaphore_signal(
            barrier, inc=1, device_id={"space": lax.rem(here + step, tiles)}, device_id_type=MESH
        )
    for neighbour in (left, right):
        pl.semaphore_signal(barrier, inc=1, device_id={"date": neighbour}, device_id_type=MESH)

    rows_each = panels_ref.shape[1]
    row = lax.broadcasted_iota(jnp.int32, panels_ref.shape[1:], 0)

    def masked(target):
        pick = jnp.int32(0)
        for i in range(tiles):
            pick = jnp.where(owner_ref[here * tiles + i] == target, i, pick)
        return jnp.where(row < valid_ref[here * tiles + pick], panels_ref[pick], 0.0)

    recv[here] = masked(here)
    for step in range(1, tiles):
        stage[step - 1] = masked(lax.rem(here + step, tiles))
    pl.semaphore_wait(barrier, tiles + 1)

    def panel_copy(step, place):
        return pltpu.make_async_remote_copy(
            src_ref=stage.at[step - 1],
            dst_ref=recv.at[place],
            send_sem=panel_send.at[step - 1],
            recv_sem=panel_recv.at[step - 1],
            device_id={"space": lax.rem(here + step, tiles)},
            device_id_type=MESH,
        )

    sends = [panel_copy(step, here) for step in range(1, tiles)]
    for send in sends:
        send.start()
    slots = []
    for source in range(tiles):
        slot = jnp.int32(0)
        for i in range(tiles):
            at = source * tiles + i
            slot = jnp.where(owner_ref[at] == here, offset_ref[at], slot)
        slots.append(slot)
    orders = []
    for target in range(tiles):
        order = jnp.int32(0)
        for source in range(tiles):
            order = jnp.where(slots[source] == target, source, order)
        orders.append(order)
    for step in range(1, tiles):
        panel_copy(step, lax.rem(here + tiles - step, tiles)).wait_recv()
    for target in range(tiles):
        image_ref[pl.ds(target * rows_each, rows_each), :] = recv[orders[target]]

    def hop(source, target, send_sem, recv_sem, c):
        return pltpu.make_async_remote_copy(
            src_ref=source.at[c],
            dst_ref=target.at[c],
            send_sem=send_sem.at[c],
            recv_sem=recv_sem.at[c],
            device_id={"date": right},
            device_id_type=MESH,
        )

    chunks = own_ref.shape[0]
    first = [hop(own_ref, one_ref, one_send, one_recv, c) for c in range(chunks)]
    second = [hop(one_ref, two_ref, two_send, two_recv, c) for c in range(chunks)]
    wallis(image_ref, own_ref, own_ref.shape[1], lambda c: first[c].start())
    for send in sends:
        send.wait_send()
    for load in loads:
        load.wait()
    ref_cols, frame_cols, ref_rows, frame_rows, back_rows, back_cols, wide, tall = held
    own = whole_of(own_ref)
    spectrum(own, ref_cols, ref_rows, ref_spec)
    ref_power[...] = powers(own, wide[1], tall[1])
    for c in range(chunks):
        first[c].wait_recv()
        second[c].start()

    for k, frame_ref in enumerate((one_ref, two_ref)):
        if k == 1:
            for c in range(chunks):
                second[c].wait_recv()
        x = whole_of(frame_ref)
        spectrum(x, frame_cols, frame_rows, frame_spec)
        frame_power[...] = powers(x, wide[0], tall[0])
        used = used_ref[k].astype(F32)
        surfaces(ref_spec, frame_spec, ref_power, frame_power, used, back_rows, back_cols, match_ref)
        arrange(match_ref, out_ref, k)
    for c in range(chunks):
        first[c].wait_send()
        second[c].wait_send()


def local(scene_panels, panel_owner, panel_offset, panel_rows, pair_used):
    tiles = lax.axis_size("space")
    dates = lax.axis_size("date")
    panels = scene_panels[0]
    rows_each = panels.shape[1]
    width = panels.shape[2]
    shifts = pair_used.shape[1]
    consts = [jnp.asarray(t) for t in tables()]
    vmem = pl.BlockSpec(memory_space=pltpu.VMEM)
    smem = pl.BlockSpec(memory_space=pltpu.SMEM)
    hbm = pl.BlockSpec(memory_space=pltpu.HBM)
    tile = pltpu.VMEM((CHUNKS, width // CHUNKS, width), BF16)
    spec = pltpu.VMEM((GROUPS, 2 * PER * HALF, GROUPS * 256), F32)
    flat = pltpu.VMEM((COUNT * UPAD, 256), F32)
    out = pl.pallas_call(
        functools.partial(kernel, tiles, dates),
        out_shape=jax.ShapeDtypeStruct((shifts, LAGS, LAGS, CHIPS), F32),
        in_specs=[smem] * 4 + [vmem] + [hbm] * TABLES,
        out_specs=vmem,
        scratch_shapes=[pltpu.VMEM(t.shape, t.dtype) for t in consts]
        + [
            pltpu.VMEM((tiles - 1, rows_each, width), F32),
            pltpu.VMEM((tiles, rows_each, width), F32),
            pltpu.VMEM((width, width), F32),
            tile,
            tile,
            tile,
            spec,
            spec,
            flat,
            flat,
            flat,
            pltpu.SemaphoreType.DMA((TABLES,)),
            pltpu.SemaphoreType.DMA((tiles - 1,)),
            pltpu.SemaphoreType.DMA((tiles - 1,)),
            pltpu.SemaphoreType.DMA((CHUNKS,)),
            pltpu.SemaphoreType.DMA((CHUNKS,)),
            pltpu.SemaphoreType.DMA((CHUNKS,)),
            pltpu.SemaphoreType.DMA((CHUNKS,)),
        ],
        compiler_params=pltpu.CompilerParams(
            vmem_limit_bytes=40 * 2**20, collective_id=0, has_side_effects=True
        ),
    )(panel_owner[0], panel_offset[0], panel_rows[0], pair_used[0], panels, *consts)
    return out[None, None]


def solution(mesh):
    placed = (
        P("date", "space", None, None),
        P("date", None),
        P("date", None),
        P("date", None),
        P("date", None),
    )
    return jax.shard_map(
        local,
        mesh=mesh,
        in_specs=placed,
        out_specs=P("date", "space", None, None, None, None),
        check_vma=False,
    )
```

```python
import functools
import math

import jax
import jax.numpy as jnp
import ml_dtypes
import numpy as np
from jax import lax
from jax.experimental import pallas as pl
from jax.experimental.pallas import tpu as pltpu
from jax.sharding import PartitionSpec as P

CHIP = 32
SEARCH = 8
WALLIS = 10
FRAME = CHIP + 2 * SEARCH
LAGS = 2 * SEARCH + 1
HALF = FRAME // 2
WALLIS_FLOOR = 0.25
MATCH_FLOOR = 0.1
TILE = 384
COUNT = TILE // CHIP
CHIPS = COUNT * COUNT
GROUPS = 3
PER = COUNT // GROUPS
UPAD = 24
FIRST = 128 // COUNT
F32 = jnp.float32
BF16 = jnp.bfloat16
MESH = pl.DeviceIdType.MESH
TABLES = 8
CHUNKS = 6

ROW_START = (0, 112, 224)
ROW_LEN = 160
COL_START = (0, 0, 128)
COL_LEN = (256, 384, 256)


def lane_of(v, cj):
    return v * COUNT + cj if v < FIRST else 128 + (v - FIRST) * COUNT + cj


def split_host(x):
    hi = x.astype(ml_dtypes.bfloat16)
    lo = (x - hi.astype(np.float64)).astype(ml_dtypes.bfloat16)
    return np.stack([hi, lo])


@functools.lru_cache(None)
def tables():
    j = np.arange(HALF)
    omega = 2.0 * math.pi * (j + 0.5) / FRAME

    def columns(lo, hi):
        out = np.zeros((TILE, GROUPS * 256))
        for cj in range(COUNT):
            g, q = divmod(cj, PER)
            for b in range(lo, hi):
                x = CHIP * cj + b - SEARCH
                if 0 <= x < TILE:
                    base = g * 256 + q * HALF
                    out[x, base : base + HALF] = np.cos(omega * (b - lo if lo else b))
                    out[x, base + 128 : base + 128 + HALF] = np.sin(omega * (b - lo if lo else b))
        return out

    def rows(lo, hi):
        out = np.zeros((GROUPS, 2 * PER * HALF, ROW_LEN))
        for ci in range(COUNT):
            h, q = divmod(ci, PER)
            for a in range(lo, hi):
                y = CHIP * ci + a - SEARCH
                if 0 <= y < TILE:
                    out[h, q * HALF : (q + 1) * HALF, y - ROW_START[h]] = np.cos(omega * (a - lo if lo else a))
                    base = PER * HALF + q * HALF
                    out[h, base : base + HALF, y - ROW_START[h]] = np.sin(omega * (a - lo if lo else a))
        return out

    back_rows = np.zeros((PER * UPAD, 2 * PER * HALF))
    for q in range(PER):
        for u in range(LAGS):
            back_rows[q * UPAD + u, q * HALF : (q + 1) * HALF] = np.cos(omega * u)
            base = PER * HALF + q * HALF
            back_rows[q * UPAD + u, base : base + HALF] = np.sin(omega * u)
    back_cols = np.zeros((GROUPS, 256, 256))
    for cj in range(COUNT):
        g, q = divmod(cj, PER)
        for v in range(LAGS):
            back_cols[g, q * HALF : (q + 1) * HALF, lane_of(v, cj)] = np.cos(omega * v)
            base = 128 + q * HALF
            back_cols[g, base : base + HALF, lane_of(v, cj)] = np.sin(omega * v)

    wide = np.zeros((2, TILE, 256))
    tall = np.zeros((2, GROUPS, PER * UPAD, ROW_LEN))
    for c in range(COUNT):
        for v in range(LAGS):
            start = CHIP * c + v - SEARCH
            wide[0, max(start, 0) : max(start + CHIP, 0), lane_of(v, c)] = 1
            h, q = divmod(c, PER)
            low, high = max(start, 0) - ROW_START[h], min(start + CHIP, TILE) - ROW_START[h]
            tall[0, h, q * UPAD + v, low:high] = 1
            wide[1, CHIP * c : CHIP * c + CHIP, lane_of(v, c)] = 1
            low = CHIP * c - ROW_START[h]
            tall[1, h, q * UPAD + v, low : low + CHIP] = 1
    return (
        split_host(columns(SEARCH, SEARCH + CHIP)),
        split_host(columns(0, FRAME)),
        split_host(rows(SEARCH, SEARCH + CHIP)),
        split_host(rows(0, FRAME)),
        split_host(back_rows),
        split_host(back_cols),
        wide.astype(ml_dtypes.bfloat16),
        tall.astype(ml_dtypes.bfloat16),
    )


def dot(a, b):
    return jnp.dot(a, b, preferred_element_type=F32)


def split(x):
    hi = x.astype(BF16)
    return hi, (x - hi.astype(F32)).astype(BF16)


def split3(x):
    hi = x.astype(BF16)
    rest = x - hi.astype(F32)
    mid = rest.astype(BF16)
    return hi, mid, (rest - mid.astype(F32)).astype(BF16)


def boxed(x, box):
    a, b, c = split3(x)
    return dot(a, box) + dot(b, box) + dot(c, box)


def banded(rows, first, size):
    i = lax.broadcasted_iota(jnp.int32, (rows, size), 0) + first
    j = lax.broadcasted_iota(jnp.int32, (rows, size), 1)
    return jnp.where(jnp.abs(i - j) <= WALLIS, 1.0, 0.0).astype(BF16)


def counts(k, size):
    return (jnp.minimum(k, WALLIS) + jnp.minimum(size - 1 - k, WALLIS) + 1).astype(F32)


def wallis(image_ref, filtered_ref, chunk, ready):
    size = image_ref.shape[0]
    image = image_ref[...]
    box = banded(size, 0, size)
    totals = split3(boxed(image, box))
    squares = split3(boxed(image * image, box))
    cols = 1.0 / counts(lax.broadcasted_iota(jnp.int32, (1, size), 1), size)
    for c in range(size // chunk):
        first = c * chunk
        part = banded(chunk, first, size)
        rows = 1.0 / counts(lax.broadcasted_iota(jnp.int32, (chunk, 1), 0) + first, size)
        inverse = rows * cols
        center = sum(dot(part, t) for t in totals) * inverse
        spread = sum(dot(part, t) for t in squares) * inverse - center * center
        at = pl.ds(first, chunk)
        filtered_ref[c] = ((image_ref[at, :] - center) * lax.rsqrt(spread + WALLIS_FLOOR)).astype(BF16)
        ready(c)


def across(x, cols_ref, wide, z_ref, e_ref, at):
    for g in range(GROUPS):
        cols = pl.ds(COL_START[g], COL_LEN[g])
        piece = x[:, COL_START[g] : COL_START[g] + COL_LEN[g]]
        lanes = pl.ds(g * 256, 256)
        hi, lo = split(dot(piece, cols_ref[0, cols, lanes]) + dot(piece, cols_ref[1, cols, lanes]))
        z_ref[0, at, lanes], z_ref[1, at, lanes] = hi, lo
    wide_f = x.astype(F32)
    hi, lo = split(wide_f * wide_f)
    hi, lo = split(dot(hi, wide) + dot(lo, wide))
    e_ref[0, at, :], e_ref[1, at, :] = hi, lo


def down(h, rows_ref, tall, z_ref, e_ref, spec, power):
    at = pl.ds(ROW_START[h], ROW_LEN)
    for g in range(GROUPS):
        lanes = pl.ds(g * 256, 256)
        zh, zl = z_ref[0, at, lanes], z_ref[1, at, lanes]
        spec[h, :, lanes] = dot(rows_ref[0, h], zh) + dot(rows_ref[0, h], zl) + dot(rows_ref[1, h], zh)
    out = pl.ds(h * PER * UPAD, PER * UPAD)
    power[out, :] = dot(tall[h], e_ref[0, at, :]) + dot(tall[h], e_ref[1, at, :])


def surfaces(group, ref_spec, frame_spec, ref_power, frame_power, used, back_rows, back_cols, match_ref):
    mid = PER * HALF
    area = float(CHIP * CHIP)
    for h in (group,):
        total = None
        for g in range(GROUPS):
            even, odd = pl.ds(g * 256, 128), pl.ds(g * 256 + 128, 128)
            top, low = pl.ds(0, mid), pl.ds(mid, mid)
            rcc, rcs = ref_spec[h, top, even], ref_spec[h, top, odd]
            rsc, rss = ref_spec[h, low, even], ref_spec[h, low, odd]
            wcc, wcs = frame_spec[h, top, even], frame_spec[h, top, odd]
            wsc, wss = frame_spec[h, low, even], frame_spec[h, low, odd]
            ap, bp, am, bm = rcc - rss, rsc + rcs, rcc + rss, rsc - rcs
            cp, dp, cm, dm = wcc - wss, wsc + wcs, wcc + wss, wsc - wcs
            pr, pi = ap * cp + bp * dp, bp * cp - ap * dp
            mr, mi = am * cm + bm * dm, bm * cm - am * dm
            upper = jnp.concatenate([pr + mr, mi - pi], axis=1)
            lower = jnp.concatenate([-(pi + mi), mr - pr], axis=1)
            hi, lo = split(jnp.concatenate([upper, lower], axis=0))
            y = dot(back_rows[0], hi) + dot(back_rows[0], lo) + dot(back_rows[1], hi)
            hi, lo = split(y)
            term = dot(hi, back_cols[0, g]) + dot(lo, back_cols[0, g]) + dot(hi, back_cols[1, g])
            total = term if total is None else total + term
        at = pl.ds(h * PER * UPAD, PER * UPAD)
        scale = 2.0 / (FRAME * FRAME) / area
        power = (ref_power[at, :] * (1.0 / area) + MATCH_FLOOR) * (frame_power[at, :] * (1.0 / area) + MATCH_FLOOR)
        match_ref[at, :] = total * (scale * used) * lax.rsqrt(power)


def arrange(match_ref, out_ref, k):
    lane = lax.broadcasted_iota(jnp.int32, (UPAD, 128), 1)
    for v in range(LAGS):
        start = lane_of(v, 0)
        tile, off = divmod(start, 128)
        first = jnp.zeros((UPAD, 128), F32)
        second = jnp.zeros((UPAD, 128), F32)
        for ci in range(COUNT):
            piece = match_ref[pl.ds(ci * UPAD, UPAD), pl.ds(tile * 128, 128)]
            turn = (COUNT * ci - off) % 128
            if turn:
                piece = pltpu.roll(piece, turn, 1)
            begin, end = COUNT * ci, COUNT * ci + COUNT
            if begin < 128:
                first = jnp.where((lane >= begin) & (lane < end), piece, first)
            if end > 128:
                second = jnp.where((lane >= begin - 128) & (lane < end - 128), piece, second)
        out_ref[k, :, v, pl.ds(0, 128)] = first[:LAGS]
        out_ref[k, :, v, pl.ds(128, CHIPS - 128)] = second[:LAGS, : CHIPS - 128]


def kernel(
    tiles, dates,
    owner_ref, offset_ref, valid_ref, used_ref, panels_ref, *refs,
):
    hbm = refs[:TABLES]
    out_ref = refs[TABLES]
    held = refs[TABLES + 1 : 2 * TABLES + 1]
    (
        stage, recv, image_ref, own_ref, one_ref, two_ref,
        ref_spec, frame_spec, ref_power, frame_power, match_ref, z_ref, e_ref,
        table_sem, panel_send, panel_recv, one_send, one_recv, two_send, two_recv,
    ) = refs[2 * TABLES + 1 :]
    here = lax.axis_index("space")
    date = lax.axis_index("date")
    right, left = lax.rem(date + 1, dates), lax.rem(date + dates - 1, dates)
    loads = [pltpu.make_async_copy(hbm[i], held[i], table_sem.at[i]) for i in range(TABLES)]
    for load in loads:
        load.start()

    barrier = pltpu.get_barrier_semaphore()
    for step in range(1, tiles):
        pl.semaphore_signal(
            barrier, inc=1, device_id={"space": lax.rem(here + step, tiles)}, device_id_type=MESH
        )
    for neighbour in (left, right):
        pl.semaphore_signal(barrier, inc=1, device_id={"date": neighbour}, device_id_type=MESH)

    rows_each = panels_ref.shape[1]
    row = lax.broadcasted_iota(jnp.int32, panels_ref.shape[1:], 0)

    def masked(target):
        pick = jnp.int32(0)
        for i in range(tiles):
            pick = jnp.where(owner_ref[here * tiles + i] == target, i, pick)
        return jnp.where(row < valid_ref[here * tiles + pick], panels_ref[pick], 0.0)

    recv[here] = masked(here)
    for step in range(1, tiles):
        stage[step - 1] = masked(lax.rem(here + step, tiles))
    pl.semaphore_wait(barrier, tiles + 1)

    def panel_copy(step, place):
        return pltpu.make_async_remote_copy(
            src_ref=stage.at[step - 1],
            dst_ref=recv.at[place],
            send_sem=panel_send.at[step - 1],
            recv_sem=panel_recv.at[step - 1],
            device_id={"space": lax.rem(here + step, tiles)},
            device_id_type=MESH,
        )

    sends = [panel_copy(step, here) for step in range(1, tiles)]
    for send in sends:
        send.start()
    slots = []
    for source in range(tiles):
        slot = jnp.int32(0)
        for i in range(tiles):
            at = source * tiles + i
            slot = jnp.where(owner_ref[at] == here, offset_ref[at], slot)
        slots.append(slot)
    orders = []
    for target in range(tiles):
        order = jnp.int32(0)
        for source in range(tiles):
            order = jnp.where(slots[source] == target, source, order)
        orders.append(order)
    for step in range(1, tiles):
        panel_copy(step, lax.rem(here + tiles - step, tiles)).wait_recv()
    for target in range(tiles):
        image_ref[pl.ds(target * rows_each, rows_each), :] = recv[orders[target]]

    def hop(source, target, send_sem, recv_sem, c):
        return pltpu.make_async_remote_copy(
            src_ref=source.at[c],
            dst_ref=target.at[c],
            send_sem=send_sem.at[c],
            recv_sem=recv_sem.at[c],
            device_id={"date": right},
            device_id_type=MESH,
        )

    chunks = own_ref.shape[0]
    first = [hop(own_ref, one_ref, one_send, one_recv, c) for c in range(chunks)]
    second = [hop(one_ref, two_ref, two_send, two_recv, c) for c in range(chunks)]
    wallis(image_ref, own_ref, own_ref.shape[1], lambda c: first[c].start())
    for send in sends:
        send.wait_send()
    for load in loads:
        load.wait()
    ref_cols, frame_cols, ref_rows, frame_rows, back_rows, back_cols, wide, tall = held
    chunk = own_ref.shape[1]
    for c in range(chunks):
        across(own_ref[c], ref_cols, wide[1], z_ref, e_ref, pl.ds(c * chunk, chunk))
    for h in range(GROUPS):
        down(h, ref_rows, tall.at[1], z_ref, e_ref, ref_spec, ref_power)
    for c in range(chunks):
        first[c].wait_recv()
        second[c].start()

    for k, frame_ref in enumerate((one_ref, two_ref)):
        used = used_ref[k].astype(F32)
        done = 0
        for c in range(chunks):
            if k == 1:
                second[c].wait_recv()
            across(frame_ref[c], frame_cols, wide[0], z_ref, e_ref, pl.ds(c * chunk, chunk))
            while done < GROUPS and ROW_START[done] + ROW_LEN <= (c + 1) * chunk:
                down(done, frame_rows, tall.at[0], z_ref, e_ref, frame_spec, frame_power)
                surfaces(
                    done, ref_spec, frame_spec, ref_power, frame_power, used, back_rows, back_cols, match_ref
                )
                done += 1
        arrange(match_ref, out_ref, k)
    for c in range(chunks):
        first[c].wait_send()
        second[c].wait_send()


def local(scene_panels, panel_owner, panel_offset, panel_rows, pair_used):
    tiles = lax.axis_size("space")
    dates = lax.axis_size("date")
    panels = scene_panels[0]
    rows_each = panels.shape[1]
    width = panels.shape[2]
    shifts = pair_used.shape[1]
    consts = [jnp.asarray(t) for t in tables()]
    vmem = pl.BlockSpec(memory_space=pltpu.VMEM)
    smem = pl.BlockSpec(memory_space=pltpu.SMEM)
    hbm = pl.BlockSpec(memory_space=pltpu.HBM)
    tile = pltpu.VMEM((CHUNKS, width // CHUNKS, width), BF16)
    spec = pltpu.VMEM((GROUPS, 2 * PER * HALF, GROUPS * 256), F32)
    flat = pltpu.VMEM((COUNT * UPAD, 256), F32)
    out = pl.pallas_call(
        functools.partial(kernel, tiles, dates),
        out_shape=jax.ShapeDtypeStruct((shifts, LAGS, LAGS, CHIPS), F32),
        in_specs=[smem] * 4 + [vmem] + [hbm] * TABLES,
        out_specs=vmem,
        scratch_shapes=[pltpu.VMEM(t.shape, t.dtype) for t in consts]
        + [
            pltpu.VMEM((tiles - 1, rows_each, width), F32),
            pltpu.VMEM((tiles, rows_each, width), F32),
            pltpu.VMEM((width, width), F32),
            tile,
            tile,
            tile,
            spec,
            spec,
            flat,
            flat,
            flat,
            pltpu.VMEM((2, width, GROUPS * 256), BF16),
            pltpu.VMEM((2, width, 256), BF16),
            pltpu.SemaphoreType.DMA((TABLES,)),
            pltpu.SemaphoreType.DMA((tiles - 1,)),
            pltpu.SemaphoreType.DMA((tiles - 1,)),
            pltpu.SemaphoreType.DMA((CHUNKS,)),
            pltpu.SemaphoreType.DMA((CHUNKS,)),
            pltpu.SemaphoreType.DMA((CHUNKS,)),
            pltpu.SemaphoreType.DMA((CHUNKS,)),
        ],
        compiler_params=pltpu.CompilerParams(
            vmem_limit_bytes=64 * 2**20 - 2**16, collective_id=0, has_side_effects=True
        ),
    )(panel_owner[0], panel_offset[0], panel_rows[0], pair_used[0], panels, *consts)
    return out[None, None]


def solution(mesh):
    placed = (
        P("date", "space", None, None),
        P("date", None),
        P("date", None),
        P("date", None),
        P("date", None),
    )
    return jax.shard_map(
        local,
        mesh=mesh,
        in_specs=placed,
        out_specs=P("date", "space", None, None, None, None),
        check_vma=False,
    )
```

```python
import functools
import math

import jax
import jax.numpy as jnp
import ml_dtypes
import numpy as np
from jax import lax
from jax.experimental import pallas as pl
from jax.experimental.pallas import tpu as pltpu
from jax.sharding import PartitionSpec as P

CHIP = 32
SEARCH = 8
WALLIS = 10
FRAME = CHIP + 2 * SEARCH
LAGS = 2 * SEARCH + 1
HALF = FRAME // 2
WALLIS_FLOOR = 0.25
MATCH_FLOOR = 0.1
TILE = 384
COUNT = TILE // CHIP
CHIPS = COUNT * COUNT
GROUPS = 3
PER = COUNT // GROUPS
UPAD = 24
FIRST = 128 // COUNT
F32 = jnp.float32
BF16 = jnp.bfloat16
MESH = pl.DeviceIdType.MESH
TABLES = 8
CHUNKS = 6

ROW_START = (0, 112, 224)
ROW_LEN = 160
COL_START = (0, 0, 128)
COL_LEN = (256, 384, 256)


def lane_of(v, cj):
    return v * COUNT + cj if v < FIRST else 128 + (v - FIRST) * COUNT + cj


def split_host(x):
    hi = x.astype(ml_dtypes.bfloat16)
    lo = (x - hi.astype(np.float64)).astype(ml_dtypes.bfloat16)
    return np.stack([hi, lo])


@functools.lru_cache(None)
def tables():
    j = np.arange(HALF)
    omega = 2.0 * math.pi * (j + 0.5) / FRAME

    def columns(lo, hi):
        out = np.zeros((TILE, GROUPS * 256))
        for cj in range(COUNT):
            g, q = divmod(cj, PER)
            for b in range(lo, hi):
                x = CHIP * cj + b - SEARCH
                if 0 <= x < TILE:
                    base = g * 256 + q * HALF
                    out[x, base : base + HALF] = np.cos(omega * (b - lo if lo else b))
                    out[x, base + 128 : base + 128 + HALF] = np.sin(omega * (b - lo if lo else b))
        return out

    def rows(lo, hi):
        out = np.zeros((GROUPS, 2 * PER * HALF, ROW_LEN))
        for ci in range(COUNT):
            h, q = divmod(ci, PER)
            for a in range(lo, hi):
                y = CHIP * ci + a - SEARCH
                if 0 <= y < TILE:
                    out[h, q * HALF : (q + 1) * HALF, y - ROW_START[h]] = np.cos(omega * (a - lo if lo else a))
                    base = PER * HALF + q * HALF
                    out[h, base : base + HALF, y - ROW_START[h]] = np.sin(omega * (a - lo if lo else a))
        return out

    back_rows = np.zeros((PER * UPAD, 2 * PER * HALF))
    for q in range(PER):
        for u in range(LAGS):
            back_rows[q * UPAD + u, q * HALF : (q + 1) * HALF] = np.cos(omega * u)
            base = PER * HALF + q * HALF
            back_rows[q * UPAD + u, base : base + HALF] = np.sin(omega * u)
    back_cols = np.zeros((GROUPS, 256, 256))
    for cj in range(COUNT):
        g, q = divmod(cj, PER)
        for v in range(LAGS):
            back_cols[g, q * HALF : (q + 1) * HALF, lane_of(v, cj)] = np.cos(omega * v)
            base = 128 + q * HALF
            back_cols[g, base : base + HALF, lane_of(v, cj)] = np.sin(omega * v)

    wide = np.zeros((2, TILE, 256))
    tall = np.zeros((2, GROUPS, PER * UPAD, ROW_LEN))
    for c in range(COUNT):
        for v in range(LAGS):
            start = CHIP * c + v - SEARCH
            wide[0, max(start, 0) : max(start + CHIP, 0), lane_of(v, c)] = 1
            h, q = divmod(c, PER)
            low, high = max(start, 0) - ROW_START[h], min(start + CHIP, TILE) - ROW_START[h]
            tall[0, h, q * UPAD + v, low:high] = 1
            wide[1, CHIP * c : CHIP * c + CHIP, lane_of(v, c)] = 1
            low = CHIP * c - ROW_START[h]
            tall[1, h, q * UPAD + v, low : low + CHIP] = 1
    return (
        split_host(columns(SEARCH, SEARCH + CHIP)),
        split_host(columns(0, FRAME)),
        split_host(rows(SEARCH, SEARCH + CHIP)),
        split_host(rows(0, FRAME)),
        split_host(back_rows),
        split_host(back_cols),
        wide.astype(ml_dtypes.bfloat16),
        tall.astype(ml_dtypes.bfloat16),
    )


def dot(a, b):
    return jnp.dot(a, b, preferred_element_type=F32)


def split(x):
    hi = x.astype(BF16)
    return hi, (x - hi.astype(F32)).astype(BF16)


def split3(x):
    hi = x.astype(BF16)
    rest = x - hi.astype(F32)
    mid = rest.astype(BF16)
    return hi, mid, (rest - mid.astype(F32)).astype(BF16)


def boxed(x, box):
    a, b, c = split3(x)
    return dot(a, box) + dot(b, box) + dot(c, box)


def banded(rows, first, size):
    i = lax.broadcasted_iota(jnp.int32, (rows, size), 0) + first
    j = lax.broadcasted_iota(jnp.int32, (rows, size), 1)
    return jnp.where(jnp.abs(i - j) <= WALLIS, 1.0, 0.0).astype(BF16)


def counts(k, size):
    return (jnp.minimum(k, WALLIS) + jnp.minimum(size - 1 - k, WALLIS) + 1).astype(F32)


def wallis(image_ref, filtered_ref, chunk, ready):
    size = image_ref.shape[0]
    image = image_ref[...]
    box = banded(size, 0, size)
    totals = split3(boxed(image, box))
    squares = split3(boxed(image * image, box))
    cols = 1.0 / counts(lax.broadcasted_iota(jnp.int32, (1, size), 1), size)
    for c in range(size // chunk):
        first = c * chunk
        low, high = max(0, first - 16), min(size, first + chunk + 16)
        part = banded(chunk, first - low, high - low)
        rows = 1.0 / counts(lax.broadcasted_iota(jnp.int32, (chunk, 1), 0) + first, size)
        inverse = rows * cols
        center = sum(dot(part, t[low:high]) for t in totals) * inverse
        spread = sum(dot(part, t[low:high]) for t in squares) * inverse - center * center
        at = pl.ds(first, chunk)
        filtered_ref[c] = ((image_ref[at, :] - center) * lax.rsqrt(spread + WALLIS_FLOOR)).astype(BF16)
        ready(c)


def across(x, cols_ref, wide, z_ref, e_ref, at):
    for g in range(GROUPS):
        cols = pl.ds(COL_START[g], COL_LEN[g])
        piece = x[:, COL_START[g] : COL_START[g] + COL_LEN[g]]
        lanes = pl.ds(g * 256, 256)
        hi, lo = split(dot(piece, cols_ref[0, cols, lanes]) + dot(piece, cols_ref[1, cols, lanes]))
        z_ref[0, at, lanes], z_ref[1, at, lanes] = hi, lo
    wide_f = x.astype(F32)
    hi, lo = split(wide_f * wide_f)
    hi, lo = split(dot(hi, wide) + dot(lo, wide))
    e_ref[0, at, :], e_ref[1, at, :] = hi, lo


def down(h, rows_ref, tall, z_ref, e_ref, spec, power):
    at = pl.ds(ROW_START[h], ROW_LEN)
    for g in range(GROUPS):
        lanes = pl.ds(g * 256, 256)
        zh, zl = z_ref[0, at, lanes], z_ref[1, at, lanes]
        spec[h, :, lanes] = dot(rows_ref[0, h], zh) + dot(rows_ref[0, h], zl) + dot(rows_ref[1, h], zh)
    out = pl.ds(h * PER * UPAD, PER * UPAD)
    power[out, :] = dot(tall[h], e_ref[0, at, :]) + dot(tall[h], e_ref[1, at, :])


def surfaces(group, ref_spec, frame_spec, ref_power, frame_power, used, back_rows, back_cols, match_ref):
    mid = PER * HALF
    area = float(CHIP * CHIP)
    for h in (group,):
        total = None
        for g in range(GROUPS):
            even, odd = pl.ds(g * 256, 128), pl.ds(g * 256 + 128, 128)
            top, low = pl.ds(0, mid), pl.ds(mid, mid)
            rcc, rcs = ref_spec[h, top, even], ref_spec[h, top, odd]
            rsc, rss = ref_spec[h, low, even], ref_spec[h, low, odd]
            wcc, wcs = frame_spec[h, top, even], frame_spec[h, top, odd]
            wsc, wss = frame_spec[h, low, even], frame_spec[h, low, odd]
            ap, bp, am, bm = rcc - rss, rsc + rcs, rcc + rss, rsc - rcs
            cp, dp, cm, dm = wcc - wss, wsc + wcs, wcc + wss, wsc - wcs
            pr, pi = ap * cp + bp * dp, bp * cp - ap * dp
            mr, mi = am * cm + bm * dm, bm * cm - am * dm
            upper = jnp.concatenate([pr + mr, mi - pi], axis=1)
            lower = jnp.concatenate([-(pi + mi), mr - pr], axis=1)
            hi, lo = split(jnp.concatenate([upper, lower], axis=0))
            y = dot(back_rows[0], hi) + dot(back_rows[0], lo) + dot(back_rows[1], hi)
            hi, lo = split(y)
            term = dot(hi, back_cols[0, g]) + dot(lo, back_cols[0, g]) + dot(hi, back_cols[1, g])
            total = term if total is None else total + term
        at = pl.ds(h * PER * UPAD, PER * UPAD)
        scale = 2.0 / (FRAME * FRAME) / area
        power = (ref_power[at, :] * (1.0 / area) + MATCH_FLOOR) * (frame_power[at, :] * (1.0 / area) + MATCH_FLOOR)
        match_ref[at, :] = total * (scale * used) * lax.rsqrt(power)


def arrange(match_ref, out_ref, k):
    lane = lax.broadcasted_iota(jnp.int32, (UPAD, 128), 1)
    for v in range(LAGS):
        start = lane_of(v, 0)
        tile, off = divmod(start, 128)
        first = jnp.zeros((UPAD, 128), F32)
        second = jnp.zeros((UPAD, 128), F32)
        for ci in range(COUNT):
            piece = match_ref[pl.ds(ci * UPAD, UPAD), pl.ds(tile * 128, 128)]
            turn = (COUNT * ci - off) % 128
            if turn:
                piece = pltpu.roll(piece, turn, 1)
            begin, end = COUNT * ci, COUNT * ci + COUNT
            if begin < 128:
                first = jnp.where((lane >= begin) & (lane < end), piece, first)
            if end > 128:
                second = jnp.where((lane >= begin - 128) & (lane < end - 128), piece, second)
        out_ref[k, :, v, pl.ds(0, 128)] = first[:LAGS]
        out_ref[k, :, v, pl.ds(128, CHIPS - 128)] = second[:LAGS, : CHIPS - 128]


def kernel(
    tiles, dates,
    owner_ref, offset_ref, valid_ref, used_ref, panels_ref, *refs,
):
    hbm = refs[:TABLES]
    out_ref = refs[TABLES]
    held = refs[TABLES + 1 : 2 * TABLES + 1]
    (
        stage, recv, image_ref, own_ref, one_ref, two_ref,
        ref_spec, frame_spec, ref_power, frame_power, match_ref, z_ref, e_ref,
        table_sem, panel_send, panel_recv, one_send, one_recv, two_send, two_recv,
    ) = refs[2 * TABLES + 1 :]
    here = lax.axis_index("space")
    date = lax.axis_index("date")
    right, left = lax.rem(date + 1, dates), lax.rem(date + dates - 1, dates)
    loads = [pltpu.make_async_copy(hbm[i], held[i], table_sem.at[i]) for i in range(TABLES)]
    for load in loads:
        load.start()

    barrier = pltpu.get_barrier_semaphore()
    for step in range(1, tiles):
        pl.semaphore_signal(
            barrier, inc=1, device_id={"space": lax.rem(here + step, tiles)}, device_id_type=MESH
        )
    for neighbour in (left, right):
        pl.semaphore_signal(barrier, inc=1, device_id={"date": neighbour}, device_id_type=MESH)

    rows_each = panels_ref.shape[1]
    row = lax.broadcasted_iota(jnp.int32, panels_ref.shape[1:], 0)

    def masked(target):
        pick = jnp.int32(0)
        for i in range(tiles):
            pick = jnp.where(owner_ref[here * tiles + i] == target, i, pick)
        return jnp.where(row < valid_ref[here * tiles + pick], panels_ref[pick], 0.0)

    recv[here] = masked(here)
    for step in range(1, tiles):
        stage[step - 1] = masked(lax.rem(here + step, tiles))
    pl.semaphore_wait(barrier, tiles + 1)

    def panel_copy(step, place):
        return pltpu.make_async_remote_copy(
            src_ref=stage.at[step - 1],
            dst_ref=recv.at[place],
            send_sem=panel_send.at[step - 1],
            recv_sem=panel_recv.at[step - 1],
            device_id={"space": lax.rem(here + step, tiles)},
            device_id_type=MESH,
        )

    sends = [panel_copy(step, here) for step in range(1, tiles)]
    for send in sends:
        send.start()
    slots = []
    for source in range(tiles):
        slot = jnp.int32(0)
        for i in range(tiles):
            at = source * tiles + i
            slot = jnp.where(owner_ref[at] == here, offset_ref[at], slot)
        slots.append(slot)
    orders = []
    for target in range(tiles):
        order = jnp.int32(0)
        for source in range(tiles):
            order = jnp.where(slots[source] == target, source, order)
        orders.append(order)
    for step in range(1, tiles):
        panel_copy(step, lax.rem(here + tiles - step, tiles)).wait_recv()
    for target in range(tiles):
        image_ref[pl.ds(target * rows_each, rows_each), :] = recv[orders[target]]

    def hop(source, target, send_sem, recv_sem, c):
        return pltpu.make_async_remote_copy(
            src_ref=source.at[c],
            dst_ref=target.at[c],
            send_sem=send_sem.at[c],
            recv_sem=recv_sem.at[c],
            device_id={"date": right},
            device_id_type=MESH,
        )

    chunks = own_ref.shape[0]
    first = [hop(own_ref, one_ref, one_send, one_recv, c) for c in range(chunks)]
    second = [hop(one_ref, two_ref, two_send, two_recv, c) for c in range(chunks)]
    wallis(image_ref, own_ref, own_ref.shape[1], lambda c: first[c].start())
    for send in sends:
        send.wait_send()
    for load in loads:
        load.wait()
    ref_cols, frame_cols, ref_rows, frame_rows, back_rows, back_cols, wide, tall = held
    chunk = own_ref.shape[1]
    for c in range(chunks):
        across(own_ref[c], ref_cols, wide[1], z_ref, e_ref, pl.ds(c * chunk, chunk))
    for h in range(GROUPS):
        down(h, ref_rows, tall.at[1], z_ref, e_ref, ref_spec, ref_power)
    for c in range(chunks):
        first[c].wait_recv()
        second[c].start()

    for k, frame_ref in enumerate((one_ref, two_ref)):
        used = used_ref[k].astype(F32)
        done = 0
        for c in range(chunks):
            if k == 1:
                second[c].wait_recv()
            across(frame_ref[c], frame_cols, wide[0], z_ref, e_ref, pl.ds(c * chunk, chunk))
            while done < GROUPS and ROW_START[done] + ROW_LEN <= (c + 1) * chunk:
                down(done, frame_rows, tall.at[0], z_ref, e_ref, frame_spec, frame_power)
                surfaces(
                    done, ref_spec, frame_spec, ref_power, frame_power, used, back_rows, back_cols, match_ref
                )
                done += 1
        arrange(match_ref, out_ref, k)
    for c in range(chunks):
        first[c].wait_send()
        second[c].wait_send()


def local(scene_panels, panel_owner, panel_offset, panel_rows, pair_used):
    tiles = lax.axis_size("space")
    dates = lax.axis_size("date")
    panels = scene_panels[0]
    rows_each = panels.shape[1]
    width = panels.shape[2]
    shifts = pair_used.shape[1]
    consts = [jnp.asarray(t) for t in tables()]
    vmem = pl.BlockSpec(memory_space=pltpu.VMEM)
    smem = pl.BlockSpec(memory_space=pltpu.SMEM)
    hbm = pl.BlockSpec(memory_space=pltpu.HBM)
    tile = pltpu.VMEM((CHUNKS, width // CHUNKS, width), BF16)
    spec = pltpu.VMEM((GROUPS, 2 * PER * HALF, GROUPS * 256), F32)
    flat = pltpu.VMEM((COUNT * UPAD, 256), F32)
    out = pl.pallas_call(
        functools.partial(kernel, tiles, dates),
        out_shape=jax.ShapeDtypeStruct((shifts, LAGS, LAGS, CHIPS), F32),
        in_specs=[smem] * 4 + [vmem] + [hbm] * TABLES,
        out_specs=vmem,
        scratch_shapes=[pltpu.VMEM(t.shape, t.dtype) for t in consts]
        + [
            pltpu.VMEM((tiles - 1, rows_each, width), F32),
            pltpu.VMEM((tiles, rows_each, width), F32),
            pltpu.VMEM((width, width), F32),
            tile,
            tile,
            tile,
            spec,
            spec,
            flat,
            flat,
            flat,
            pltpu.VMEM((2, width, GROUPS * 256), BF16),
            pltpu.VMEM((2, width, 256), BF16),
            pltpu.SemaphoreType.DMA((TABLES,)),
            pltpu.SemaphoreType.DMA((tiles - 1,)),
            pltpu.SemaphoreType.DMA((tiles - 1,)),
            pltpu.SemaphoreType.DMA((CHUNKS,)),
            pltpu.SemaphoreType.DMA((CHUNKS,)),
            pltpu.SemaphoreType.DMA((CHUNKS,)),
            pltpu.SemaphoreType.DMA((CHUNKS,)),
        ],
        compiler_params=pltpu.CompilerParams(
            vmem_limit_bytes=64 * 2**20 - 2**16, collective_id=0, has_side_effects=True
        ),
    )(panel_owner[0], panel_offset[0], panel_rows[0], pair_used[0], panels, *consts)
    return out[None, None]


def solution(mesh):
    placed = (
        P("date", "space", None, None),
        P("date", None),
        P("date", None),
        P("date", None),
        P("date", None),
    )
    return jax.shard_map(
        local,
        mesh=mesh,
        in_specs=placed,
        out_specs=P("date", "space", None, None, None, None),
        check_vma=False,
    )
```
